128 devices in a mesh: rows: 8 (over x, z_hi), ci: 4 (over z_lo, core), cj: 4 (over y).
Axes of the slice: x: 4, y: 4, z: 4 (z_hi: 2, z_lo: 2; z = z_hi * 2 + z_lo), core: 2. Of those that a mesh axis runs over, the one named last changes fastest.
Arguments:
- matrix: float32 [2048, 49152], P('rows', ('ci', 'cj')), may hold values from -585 to 585
- sample: int32 [4, 4, 2048], P('ci', None, 'rows'), may hold values 0 or 1
Outputs:
- cosine: float32 [4, 12288, 4, 384], P('ci', 'rows', 'cj')
The draws below stay inside these ranges and needn't reach their ends.
All inputs are finite; a program needn't handle non-finite values. No bound on the sum of `sample` on one device may be relied on, other than what follows from the above.
Results may differ from the reference program's by a relative error of at most 0.000054.
Values sent between devices are 32-bit elements; how exact they have to be, the bound alone decides.
No kernel may reach another device: no remote copies, remote signals or barrier semaphores. Data moves between devices by JAX's collectives and lax.ppermute only.
A program may use at most 128 MiB of HBM per device.

```python
import math
import jax
import jax.numpy as jnp
from jax import lax

COLUMNS = 49152
TOTAL_ROWS = 2048
SLAB = 3072
BLOCK = 12288
QSLAB = 96
QGROUP = 384
N_CI = 4
N_CJ = 4


def draw_matrix(key, part):
    keys = jax.random.split(jax.random.fold_in(key, 17), 4)
    position = jnp.arange(TOTAL_ROWS, dtype=jnp.float32)
    rising = 1.0 + 2.0 * position / TOTAL_ROWS
    col_scale = jnp.exp(jax.random.uniform(keys[1], (COLUMNS,), jnp.float32, 0.0, math.log(10.0)))
    shared = jnp.clip(jax.random.normal(keys[2], (TOTAL_ROWS,), jnp.float32), -4.0, 4.0)
    loading = jax.random.uniform(keys[3], (COLUMNS,), jnp.float32, -1.2, 1.2)
    noise = jnp.clip(jax.random.normal(keys[0], (TOTAL_ROWS, COLUMNS), jnp.float32), -6.0, 6.0)
    return rising[:, None] * (noise + shared[:, None] * loading[None, :]) * col_scale[None, :]


def with_ends(values, own_key, smallest, high):
    longest = values.shape.index(max(values.shape))
    spots = []
    for shift in (0, 1):
        where = [jax.random.randint(jax.random.fold_in(own_key, axis), (), 0, length) for axis, length in enumerate(values.shape)]
        where[longest] = (where[longest] + shift) % values.shape[longest]
        spots.append(tuple(where))
    return values.at[spots[0]].set(smallest).at[spots[1]].set(high)


def setup_inputs(seed: int = 0) -> dict:
    seeds = jax.random.split(jax.random.key(seed), 3)
    return {
        "matrix": draw_matrix(jax.random.fold_in(seeds[2], 71), 0),
        "sample": with_ends((jax.random.randint(seeds[1], (N_CI, N_CJ, TOTAL_ROWS), 0, 2) < 1).astype(jnp.int32), jax.random.fold_in(seeds[1], 1), 0, 1),
    }


EPS = 1e-06
KEEP = 2.0

def reference(matrix, sample):
    inverse = 1.0 / jnp.sqrt(lax.optimization_barrier(jnp.sum(matrix * matrix, axis=0)) + EPS)
    unit = matrix * inverse[None, :]
    query = unit.reshape(TOTAL_ROWS, N_CI, N_CJ, SLAB)[:, :, :, :QSLAB]
    query = jnp.transpose(query, (0, 2, 1, 3)).reshape(TOTAL_ROWS, N_CJ, QGROUP) * KEEP
    blocks = unit.reshape(TOTAL_ROWS, N_CI, BLOCK)

    def one_block(index):
        columns = lax.dynamic_index_in_dim(blocks, index, 1, keepdims=False)
        picks = lax.dynamic_index_in_dim(sample, index, 0, keepdims=False).astype(jnp.float32)
        masked = query * jnp.transpose(picks)[:, :, None]
        product = jnp.dot(jnp.transpose(columns), masked.reshape(TOTAL_ROWS, N_CJ * QGROUP), precision=lax.Precision.HIGHEST, preferred_element_type=jnp.float32)
        return product.reshape(BLOCK, N_CJ, QGROUP)
    return lax.map(one_block, jnp.arange(N_CI, dtype=jnp.int32))
```

```python
import functools

import jax
import jax.numpy as jnp
from jax import lax
from jax.experimental import pallas as pl
from jax.experimental.pallas import tpu as pltpu
from jax.sharding import Mesh, PartitionSpec as P

EPS = 1e-6
LIFT = 2.0**40
AXES = ("x", "zh", "zl", "core", "y")
SIZES = (4, 2, 2, 2, 4)
ROWS, COLS, HALF, QS, GROUP = 256, 3072, 1536, 96, 384
CHUNK, TILE = 768, 256
F32, BF16 = jnp.float32, jnp.bfloat16


def pair(k, c):
    return k + 1 - 2 * (k % 2) if c == 0 else 3 - k


def mate(k, c):
    return 3 - k if c == 0 else k + 1 - 2 * (k % 2)


def moved(array, to):
    table = []
    for x in range(4):
        for zh in range(2):
            for zl in range(2):
                for c in range(2):
                    for y in range(4):
                        n = [v % s for v, s in zip(to(x, zh, zl, c, y), SIZES)]
                        table.append((x, zh, zl, c, y, n))
    def index(x, zh, zl, c, y):
        return (((x * 2 + zh) * 2 + zl) * 2 + c) * 4 + y
    return lax.ppermute(array, AXES, [(index(*t[:5]), index(*t[5])) for t in table])


def along_z(shift):
    def to(x, zh, zl, c, y):
        z = (zh * 2 + zl + shift) % 4
        return x, z // 2, z % 2, c, y
    return to


def split(v):
    hi = v.astype(BF16)
    return hi, (v - hi.astype(F32)).astype(BF16)


def query_kernel(idx_ref, pieces_ref, sample_ref, hi_ref, lo_ref, squares_ref):
    for g in range(2):
        total = [jnp.zeros((QS, 128), F32) for _ in range(4)]
        for b in range(8):
            half = (b // 2) % 2
            picks = sample_ref[idx_ref[32 + b * 2 + g]][:, half * 128 : half * 128 + 128]
            scale = picks.astype(F32) * LIFT
            for i in range(4):
                piece = pieces_ref[idx_ref[b * 4 + i] + g]
                total[i] = total[i] + piece * piece
                hi, lo = split(piece * scale)
                at = g * GROUP + i * QS
                hi_ref[at : at + QS, b * 128 : b * 128 + 128] = hi
                lo_ref[at : at + QS, b * 128 : b * 128 + 128] = lo
        for i in range(4):
            squares_ref[g, i * QS : i * QS + QS, :] = total[i]


def product_kernel(hi_ref, lo_ref, *refs):
    blocks, (own_ref, other_ref, colhi, collo) = refs[:8], refs[8:]
    squares = jnp.zeros((128, TILE), F32)
    for b, ref in enumerate(blocks):
        v = ref[...]
        squares = squares + v * v
        colhi[b * 128 : b * 128 + 128, :], collo[b * 128 : b * 128 + 128, :] = split(v)
    dot = functools.partial(jnp.dot, preferred_element_type=F32)
    for g, out in ((1, other_ref), (0, own_ref)):
        hi, lo = hi_ref[g * GROUP : (g + 1) * GROUP, :], lo_ref[g * GROUP : (g + 1) * GROUP, :]
        out[:GROUP, :] = dot(hi, colhi[...]) + (dot(hi, collo[...]) + dot(lo, colhi[...]))
        out[GROUP:, :] = jnp.broadcast_to(jnp.sum(squares, axis=0, keepdims=True), (8, TILE))


def final_kernel(own0, got0, own1, got1, sq_own, sq_got, out_ref):
    def write(own, got):
        squares = own[GROUP : GROUP + 1, :] + got[GROUP : GROUP + 1, :]
        inverse = 1.0 / jnp.sqrt(squares + EPS)
        qsquares = jnp.sum(sq_own[...] + sq_got[...], axis=1, keepdims=True)
        qinverse = (2.0 / LIFT) / jnp.sqrt(qsquares + EPS)
        value = (own[:GROUP, :] + got[:GROUP, :]) * qinverse * inverse
        for part in range(TILE // 128):
            for j in range(3):
                block = value[j * 128 : j * 128 + 128, part * 128 : part * 128 + 128]
                out_ref[pl.ds(part * 384 + j, 128, stride=3), :] = block.T

    @pl.when(pl.program_id(0) < CHUNK // TILE)
    def _():
        write(own0, got0)

    @pl.when(pl.program_id(0) >= CHUNK // TILE)
    def _():
        write(own1, got1)


def limit(mib=48):
    return pltpu.CompilerParams(vmem_limit_bytes=mib * 2**20)


def shards(matrix, sample):
    ix, ih, il, ic, iy = (lax.axis_index(a) for a in AXES)
    iz = ih * 2 + il
    my_pair = jnp.where(ic == 0, pair(iy, 0), pair(iy, 1))
    my_mate = jnp.where(ic == 0, mate(iy, 0), mate(iy, 1))

    picks = lax.all_gather(sample[0], ("x", "zh"), axis=0, tiled=False)

    own = lax.dynamic_slice(matrix, (0, ih * HALF), (ROWS, HALF))
    away = lax.dynamic_slice(matrix, (0, (1 - ih) * HALF), (ROWS, HALF))
    flip = lambda x, zh, zl, c, y: (x, 1 - zh, zl, c, y)
    got = [moved(away[:, n * CHUNK : (n + 1) * CHUNK], flip) for n in range(2)]

    def spread(rows):
        result = []
        for n in range(2):
            part = rows[n * 128 : n * 128 + 128]
            part = moved(part, lambda x, zh, zl, c, y: (x, zh, zl, c, y + x + 2 * n))
            result.append(moved(part, lambda x, zh, zl, c, y: (y - x - 2 * n, zh, zl, c, y)))
        return result

    def paired(parts):
        return [moved(p, lambda x, zh, zl, c, y: (x, zh, zl, c, pair(y, c))) for p in parts]

    mine = spread(own)
    mine = mine + paired(mine)
    others = [spread(g) for g in got]
    others = [o + paired(o) for o in others]

    raw = jnp.transpose(matrix[:, :QS])
    raw = jnp.stack(
        [
            raw,
            moved(raw, lambda x, zh, zl, c, y: (x, zh, zl, c, mate(y, 0))),
            moved(raw, lambda x, zh, zl, c, y: (x, zh, zl, c, mate(y, 1))),
        ]
    )
    raw = jnp.stack(
        [raw] + [moved(raw, lambda x, zh, zl, c, y, d=d: (x - d, zh, zl, c, y)) for d in (1, 2, 3)]
    )
    near = (ix + jnp.arange(4)) % 4

    def slot(core):
        p = pair(iy, core)
        first = (near == (iy - ix) % 4) | (near == (p - ix) % 4)
        groups = jnp.stack([raw[:, 0], raw[:, 1 + core]], axis=1)
        return jnp.where(first[:, None, None, None], groups[..., :128], groups[..., 128:])

    slots = slot(0), slot(1)
    keep = jnp.where(ic == 0, slots[0], slots[1])
    give = jnp.where(ic == 0, slots[1], slots[0])
    both = jnp.stack([keep, moved(give, lambda x, zh, zl, c, y: (x, zh, zl, 1 - c, y))])
    pieces = jnp.stack([both] + [moved(both, along_z(-d)) for d in (1, 2, 3)])
    pieces = pieces.reshape(64, QS, 128)

    block_x = jnp.stack([iy - ix, iy - ix + 2, my_pair - ix, my_pair - ix + 2]) % 4
    block_x = jnp.repeat(block_x, 2)
    block_zh = jnp.tile(jnp.stack([ih, 1 - ih]), 4)
    zl = jnp.array([0, 0, 1, 1])[None, :]
    core = jnp.array([0, 1, 0, 1])[None, :]
    dz = (block_zh[:, None] * 2 + zl - iz) % 4
    dx = (block_x[:, None] - ix) % 4
    where = ((dz * 2 + (core ^ ic)) * 4 + dx) * 2
    pick_at = (block_x * 2 + block_zh)[:, None] * 4 + jnp.stack([iy, my_mate])[None, :]
    idx = jnp.concatenate([where.reshape(-1), pick_at.reshape(-1)]).astype(jnp.int32)

    vmem = pl.BlockSpec(memory_space=pltpu.VMEM)
    qhi, qlo, qsquares = pl.pallas_call(
        query_kernel,
        out_shape=(
            jax.ShapeDtypeStruct((2 * GROUP, 1024), BF16),
            jax.ShapeDtypeStruct((2 * GROUP, 1024), BF16),
            jax.ShapeDtypeStruct((2, GROUP, 128), F32),
        ),
        in_specs=[pl.BlockSpec(memory_space=pltpu.SMEM), vmem, vmem],
        out_specs=(vmem, vmem, vmem),
        compiler_params=limit(),
        name="query_prepare",
    )(idx, pieces, picks.reshape(32, 1, ROWS))

    to_mate = lambda x, zh, zl, c, y: (x, zh, zl, c, mate(y, c))
    qsquares_got = moved(qsquares[1], to_mate)

    tiles = CHUNK // TILE
    whole = pl.BlockSpec((2 * GROUP, 1024), lambda t: (0, 0))
    ends = []
    for n in range(2):
        operands, specs = [], []
        for p in range(4):
            operands += [mine[p], others[n][p]]
            specs += [
                pl.BlockSpec((128, TILE), lambda t, n=n: (0, n * tiles + t)),
                pl.BlockSpec((128, TILE), lambda t: (0, t)),
            ]
        ours, theirs = pl.pallas_call(
            product_kernel,
            grid=(tiles,),
            out_shape=(jax.ShapeDtypeStruct((GROUP + 8, CHUNK), F32),) * 2,
            in_specs=[whole, whole] + specs,
            out_specs=(pl.BlockSpec((GROUP + 8, TILE), lambda t: (0, t)),) * 2,
            scratch_shapes=[pltpu.VMEM((1024, TILE), BF16), pltpu.VMEM((1024, TILE), BF16)],
            compiler_params=limit(),
            name="product",
        )(qhi, qlo, *operands)
        ends += [ours, moved(theirs, to_mate)]

    low = pl.BlockSpec((GROUP + 8, TILE), lambda t: (0, jnp.minimum(t, tiles - 1)))
    high = pl.BlockSpec((GROUP + 8, TILE), lambda t: (0, jnp.maximum(t - tiles, 0)))
    flat = pl.BlockSpec((GROUP, 128), lambda t: (0, 0))
    result = pl.pallas_call(
        final_kernel,
        grid=(2 * tiles,),
        out_shape=jax.ShapeDtypeStruct((HALF * 3, 128), F32),
        in_specs=[low, low, high, high, flat, flat],
        out_specs=pl.BlockSpec((TILE * 3, 128), lambda t: (t, 0)),
        compiler_params=limit(),
        name="scale_and_turn",
    )(*ends, qsquares[0], qsquares_got)
    return result.reshape(1, HALF, 1, GROUP)


def solution(mesh):
    fine = Mesh(mesh.devices.reshape(SIZES), AXES)
    rows, ci = ("x", "zh"), ("zl", "core")
    return jax.shard_map(
        shards,
        mesh=fine,
        in_specs=(P(rows, ci + ("y",)), P(ci, None, rows)),
        out_specs=P(ci, rows, "y", None),
        check_vma=False,
    )
```

```python
import functools

import jax
import jax.numpy as jnp
from jax import lax
from jax.experimental import pallas as pl
from jax.experimental.pallas import tpu as pltpu
from jax.sharding import Mesh, PartitionSpec as P

EPS = 1e-6
LIFT = 2.0**40
AXES = ("x", "zh", "zl", "core", "y")
SIZES = (4, 2, 2, 2, 4)
ROWS, COLS, HALF, QS, GROUP = 256, 3072, 1536, 96, 384
CHUNK, TILE = 768, 256
F32, BF16 = jnp.float32, jnp.bfloat16


def pair(k, c):
    return k + 1 - 2 * (k % 2) if c == 0 else 3 - k


def mate(k, c):
    return 3 - k if c == 0 else k + 1 - 2 * (k % 2)


def moved(array, to):
    table = []
    for x in range(4):
        for zh in range(2):
            for zl in range(2):
                for c in range(2):
                    for y in range(4):
                        n = [v % s for v, s in zip(to(x, zh, zl, c, y), SIZES)]
                        table.append((x, zh, zl, c, y, n))
    def index(x, zh, zl, c, y):
        return (((x * 2 + zh) * 2 + zl) * 2 + c) * 4 + y
    return lax.ppermute(array, AXES, [(index(*t[:5]), index(*t[5])) for t in table])


def along_z(shift):
    def to(x, zh, zl, c, y):
        z = (zh * 2 + zl + shift) % 4
        return x, z // 2, z % 2, c, y
    return to


def split(v):
    hi = v.astype(BF16)
    return hi, (v - hi.astype(F32)).astype(BF16)


def query_kernel(idx_ref, pieces_ref, sample_ref, hi_ref, lo_ref, squares_ref):
    for g in range(2):
        total = [jnp.zeros((QS, 128), F32) for _ in range(4)]
        for b in range(8):
            half = (b // 2) % 2
            picks = sample_ref[idx_ref[32 + b * 2 + g]][:, half * 128 : half * 128 + 128]
            scale = picks * LIFT
            for i in range(4):
                piece = pieces_ref[idx_ref[b * 4 + i] + g]
                total[i] = total[i] + piece * piece
                hi, lo = split(piece * scale)
                at = g * GROUP + i * QS
                hi_ref[at : at + QS, b * 128 : b * 128 + 128] = hi
                lo_ref[at : at + QS, b * 128 : b * 128 + 128] = lo
        for i in range(4):
            squares_ref[g, i * QS : i * QS + QS, :] = total[i]


def product_kernel(hi_ref, lo_ref, *refs):
    blocks, (own_ref, other_ref, colhi, collo) = refs[:8], refs[8:]
    squares = jnp.zeros((128, TILE), F32)
    for b, ref in enumerate(blocks):
        v = ref[...]
        squares = squares + v * v
        colhi[b * 128 : b * 128 + 128, :], collo[b * 128 : b * 128 + 128, :] = split(v)
    dot = functools.partial(jnp.dot, preferred_element_type=F32)
    for g, out in ((1, other_ref), (0, own_ref)):
        hi, lo = hi_ref[g * GROUP : (g + 1) * GROUP, :], lo_ref[g * GROUP : (g + 1) * GROUP, :]
        out[:GROUP, :] = dot(hi, colhi[...]) + (dot(hi, collo[...]) + dot(lo, colhi[...]))
        out[GROUP:, :] = jnp.broadcast_to(jnp.sum(squares, axis=0, keepdims=True), (8, TILE))


def final_kernel(own0, got0, own1, got1, sq_own, sq_got, out_ref):
    def write(own, got):
        squares = own[GROUP : GROUP + 1, :] + got[GROUP : GROUP + 1, :]
        inverse = 1.0 / jnp.sqrt(squares + EPS)
        qsquares = jnp.sum(sq_own[...] + sq_got[...], axis=1, keepdims=True)
        qinverse = (2.0 / LIFT) / jnp.sqrt(qsquares + EPS)
        value = (own[:GROUP, :] + got[:GROUP, :]) * qinverse * inverse
        for part in range(TILE // 128):
            for j in range(3):
                block = value[j * 128 : j * 128 + 128, part * 128 : part * 128 + 128]
                out_ref[pl.ds(part * 384 + j, 128, stride=3), :] = block.T

    @pl.when(pl.program_id(0) < CHUNK // TILE)
    def _():
        write(own0, got0)

    @pl.when(pl.program_id(0) >= CHUNK // TILE)
    def _():
        write(own1, got1)


def limit(mib=48):
    return pltpu.CompilerParams(vmem_limit_bytes=mib * 2**20)


def shards(matrix, sample):
    ix, ih, il, ic, iy = (lax.axis_index(a) for a in AXES)
    iz = ih * 2 + il
    my_pair = jnp.where(ic == 0, pair(iy, 0), pair(iy, 1))
    my_mate = jnp.where(ic == 0, mate(iy, 0), mate(iy, 1))

    def half_of(side):
        return lax.dynamic_slice(matrix, (0, side * HALF), (ROWS, HALF))

    def spread(rows, flip):
        result = []
        for n in range(2):
            part = rows[n * 128 : n * 128 + 128]
            part = moved(part, lambda x, zh, zl, c, y: (x, zh, zl, c, y + x + 2 * n))
            result.append(
                moved(part, lambda x, zh, zl, c, y: (y - x - 2 * n, zh + flip, zl, c, y))
            )
        return result

    def paired(parts):
        return [moved(p, lambda x, zh, zl, c, y: (x, zh, zl, c, pair(y, c))) for p in parts]

    others = spread(half_of(1 - ih), 1)
    others = others + paired(others)
    mine = spread(half_of(ih), 0)
    mine = mine + paired(mine)

    raw = jnp.transpose(matrix[:, :QS])
    picks = sample[0].astype(F32)
    raw = jnp.concatenate(
        [
            raw,
            moved(raw, lambda x, zh, zl, c, y: (x, zh, zl, c, mate(y, 0))),
            moved(raw, lambda x, zh, zl, c, y: (x, zh, zl, c, mate(y, 1))),
            picks,
            moved(picks, lambda x, zh, zl, c, y: (x, 1 - zh, zl, c, y)),
        ]
    )
    raw = jnp.stack(
        [raw] + [moved(raw, lambda x, zh, zl, c, y, d=d: (x - d, zh, zl, c, y)) for d in (1, 2, 3)]
    )
    picks = raw[:, 3 * QS :].reshape(32, 1, ROWS)
    raw = raw[:, : 3 * QS].reshape(4, 3, QS, ROWS)
    near = (ix + jnp.arange(4)) % 4

    def slot(core):
        p = pair(iy, core)
        first = (near == (iy - ix) % 4) | (near == (p - ix) % 4)
        groups = jnp.stack([raw[:, 0], raw[:, 1 + core]], axis=1)
        return jnp.where(first[:, None, None, None], groups[..., :128], groups[..., 128:])

    slots = slot(0), slot(1)
    keep = jnp.where(ic == 0, slots[0], slots[1])
    give = jnp.where(ic == 0, slots[1], slots[0])
    both = jnp.stack([keep, moved(give, lambda x, zh, zl, c, y: (x, zh, zl, 1 - c, y))])
    pieces = jnp.stack([both] + [moved(both, along_z(-d)) for d in (1, 2, 3)])
    pieces = pieces.reshape(64, QS, 128)

    block_x = jnp.stack([iy - ix, iy - ix + 2, my_pair - ix, my_pair - ix + 2]) % 4
    block_x = jnp.repeat(block_x, 2)
    block_zh = jnp.tile(jnp.stack([ih, 1 - ih]), 4)
    zl = jnp.array([0, 0, 1, 1])[None, :]
    core = jnp.array([0, 1, 0, 1])[None, :]
    dz = (block_zh[:, None] * 2 + zl - iz) % 4
    dx = (block_x[:, None] - ix) % 4
    where = ((dz * 2 + (core ^ ic)) * 4 + dx) * 2
    pick_at = (dx * 2 + jnp.arange(8)[:, None] % 2) * 4 + jnp.stack([iy, my_mate])[None, :]
    idx = jnp.concatenate([where.reshape(-1), pick_at.reshape(-1)]).astype(jnp.int32)

    vmem = pl.BlockSpec(memory_space=pltpu.VMEM)
    qhi, qlo, qsquares = pl.pallas_call(
        query_kernel,
        out_shape=(
            jax.ShapeDtypeStruct((2 * GROUP, 1024), BF16),
            jax.ShapeDtypeStruct((2 * GROUP, 1024), BF16),
            jax.ShapeDtypeStruct((2, GROUP, 128), F32),
        ),
        in_specs=[pl.BlockSpec(memory_space=pltpu.SMEM), vmem, vmem],
        out_specs=(vmem, vmem, vmem),
        compiler_params=limit(),
        name="query_prepare",
    )(idx, pieces, picks)

    to_mate = lambda x, zh, zl, c, y: (x, zh, zl, c, mate(y, c))
    qsquares_got = moved(qsquares[1], to_mate)

    tiles = CHUNK // TILE
    whole = pl.BlockSpec((2 * GROUP, 1024), lambda t: (0, 0))
    ends = []
    for n in range(2):
        operands, specs = [], []
        for p in range(4):
            operands += [mine[p], others[p]]
            specs += [pl.BlockSpec((128, TILE), lambda t, n=n: (0, n * tiles + t))] * 2
        ours, theirs = pl.pallas_call(
            product_kernel,
            grid=(tiles,),
            out_shape=(jax.ShapeDtypeStruct((GROUP + 8, CHUNK), F32),) * 2,
            in_specs=[whole, whole] + specs,
            out_specs=(pl.BlockSpec((GROUP + 8, TILE), lambda t: (0, t)),) * 2,
            scratch_shapes=[pltpu.VMEM((1024, TILE), BF16), pltpu.VMEM((1024, TILE), BF16)],
            compiler_params=limit(),
            name="product",
        )(qhi, qlo, *operands)
        ends += [ours, moved(theirs, to_mate)]

    low = pl.BlockSpec((GROUP + 8, TILE), lambda t: (0, jnp.minimum(t, tiles - 1)))
    high = pl.BlockSpec((GROUP + 8, TILE), lambda t: (0, jnp.maximum(t - tiles, 0)))
    flat = pl.BlockSpec((GROUP, 128), lambda t: (0, 0))
    result = pl.pallas_call(
        final_kernel,
        grid=(2 * tiles,),
        out_shape=jax.ShapeDtypeStruct((HALF * 3, 128), F32),
        in_specs=[low, low, high, high, flat, flat],
        out_specs=pl.BlockSpec((TILE * 3, 128), lambda t: (t, 0)),
        compiler_params=limit(),
        name="scale_and_turn",
    )(*ends, qsquares[0], qsquares_got)
    return result.reshape(1, HALF, 1, GROUP)


def solution(mesh):
    fine = Mesh(mesh.devices.reshape(SIZES), AXES)
    rows, ci = ("x", "zh"), ("zl", "core")
    return jax.shard_map(
        shards,
        mesh=fine,
        in_specs=(P(rows, ci + ("y",)), P(ci, None, rows)),
        out_specs=P(ci, rows, "y", None),
        check_vma=False,
    )
```

```python
import functools

import jax
import jax.numpy as jnp
from jax import lax
from jax.experimental import pallas as pl
from jax.experimental.pallas import tpu as pltpu
from jax.sharding import Mesh, PartitionSpec as P

EPS = 1e-6
LIFT = 2.0**40
AXES = ("x", "zh", "zl", "core", "y")
SIZES = (4, 2, 2, 2, 4)
ROWS, COLS, HALF, QS, GROUP = 256, 3072, 1536, 96, 384
CHUNK, TILE = 768, 256
F32, BF16 = jnp.float32, jnp.bfloat16


def pair(k, c):
    return k + 1 - 2 * (k % 2) if c == 0 else 3 - k


def mate(k, c):
    return 3 - k if c == 0 else k + 1 - 2 * (k % 2)


def moved(array, to):
    table = []
    for x in range(4):
        for zh in range(2):
            for zl in range(2):
                for c in range(2):
                    for y in range(4):
                        n = [v % s for v, s in zip(to(x, zh, zl, c, y), SIZES)]
                        table.append((x, zh, zl, c, y, n))
    def index(x, zh, zl, c, y):
        return (((x * 2 + zh) * 2 + zl) * 2 + c) * 4 + y
    return lax.ppermute(array, AXES, [(index(*t[:5]), index(*t[5])) for t in table])


def split(v):
    hi = v.astype(BF16)
    return hi, (v - hi.astype(F32)).astype(BF16)


def query_kernel(at_ref, pieces_ref, hilo_ref, norms_ref, squares_ref):
    total = [[jnp.zeros((QS, 128), F32) for _ in range(4)] for _ in range(2)]
    for b in range(8):
        x, zh = at_ref[b], at_ref[8 + b]
        for g in range(2):
            row = pl.multiple_of(8 * QS + (x * 4 + at_ref[16 + g]) * 8, 8)
            picks = pieces_ref[zh * 4 + at_ref[18], pl.ds(row, 8), :]
            picks = picks[b % 2 : b % 2 + 1, :] * LIFT
            for i in range(4):
                row = pl.multiple_of((x * 2 + g) * QS, 8)
                piece = pieces_ref[zh * 4 + i, pl.ds(row, QS), :]
                total[g][i] = total[g][i] + piece * piece
                hi, lo = split(piece * picks)
                to = g * GROUP + i * QS
                hilo_ref[to : to + QS, b * 128 : b * 128 + 128] = hi
                to += 2 * GROUP
                hilo_ref[to : to + QS, b * 128 : b * 128 + 128] = lo
    norms_ref[...] = jnp.zeros_like(norms_ref)
    for g in range(2):
        for i in range(4):
            squares_ref[i * QS : i * QS + QS, :] = total[g][i]
        for j in range(3):
            part = squares_ref[j * 128 : j * 128 + 128, :].T
            norms_ref[g, j + 1 : j + 2, :] = jnp.sum(part, axis=0, keepdims=True)


def products(hilo_ref, blocks, colhi, collo):
    squares = jnp.zeros((128, TILE), F32)
    for b, ref in enumerate(blocks):
        v = ref[...]
        squares = squares + v * v
        colhi[b * 128 : b * 128 + 128, :], collo[b * 128 : b * 128 + 128, :] = split(v)
    dot = functools.partial(jnp.dot, preferred_element_type=F32)
    both = dot(hilo_ref[...], colhi[...])
    value = both[: 2 * GROUP, :] + (both[2 * GROUP :, :] + dot(hilo_ref[: 2 * GROUP, :], collo[...]))
    return value, jnp.sum(squares, axis=0, keepdims=True)


def first_kernel(hilo_ref, *refs):
    blocks, (out_ref, colhi, collo) = refs[:4], refs[4:]
    value, squares = products(hilo_ref, blocks, colhi, collo)
    out_ref[: 2 * GROUP, :] = value
    out_ref[2 * GROUP :, :] = jnp.broadcast_to(squares, (8, TILE))


def second_kernel(hilo_ref, norms_ref, before_ref, *refs):
    blocks, (own_ref, other_ref, colhi, collo) = refs[:4], refs[4:]
    value, squares = products(hilo_ref, blocks, colhi, collo)
    squares = before_ref[2 * GROUP :, :] + squares
    row = lax.broadcasted_iota(jnp.int32, (8, TILE), 0)
    for g, out in ((0, own_ref), (1, other_ref)):
        here = slice(g * GROUP, (g + 1) * GROUP)
        out[:GROUP, :] = before_ref[here, :] + value[here, :]
        norms = jnp.concatenate([norms_ref[g]] * (TILE // 128), axis=1)
        out[GROUP:, :] = jnp.where(row == 0, squares, norms)


def final_kernel(own, got, *refs):
    out_ref = refs[-1]
    squares = own[GROUP:, :] + got[GROUP:, :]
    inverse = 1.0 / jnp.sqrt(squares[:1, :] + EPS)
    value = (own[:GROUP, :] + got[:GROUP, :]) * inverse
    for j in range(3):
        scale = (2.0 / LIFT) / jnp.sqrt(squares[j + 1 : j + 2, :128] + EPS)
        for part in range(TILE // 128):
            block = value[j * 128 : j * 128 + 128, part * 128 : part * 128 + 128]
            out_ref[pl.ds(part * 384 + j, 128, stride=3), :] = block.T * scale


def limit(mib=48):
    return pltpu.CompilerParams(vmem_limit_bytes=mib * 2**20)


def shards(matrix, sample):
    ix, ih, il, ic, iy = (lax.axis_index(a) for a in AXES)
    my_pair = jnp.where(ic == 0, pair(iy, 0), pair(iy, 1))
    my_mate = jnp.where(ic == 0, mate(iy, 0), mate(iy, 1))

    def half_of(side):
        return lax.dynamic_slice(matrix, (0, side * HALF), (ROWS, HALF))

    def first_step(part, n):
        return moved(part, lambda x, zh, zl, c, y: (x, zh, zl, c, y + x + 2 * n))

    def second_step(part, n):
        return moved(part, lambda x, zh, zl, c, y: (y - x - 2 * n, zh, zl, c, y))

    def paired(parts):
        return [moved(p, lambda x, zh, zl, c, y: (x, zh, zl, c, pair(y, c))) for p in parts]

    near, away = half_of(ih), half_of(1 - ih)
    away = moved(away, lambda x, zh, zl, c, y: (x, 1 - zh, zl, c, y))

    raw = jnp.transpose(matrix[:, :QS])
    mates = [moved(raw, lambda x, zh, zl, c, y, k=k: (x, zh, zl, c, mate(y, k))) for k in (0, 1)]
    mates, near = lax.optimization_barrier((mates, near))
    raw = jnp.concatenate([raw, *mates, sample[0].astype(F32), jnp.zeros((4, ROWS), F32)])
    raw = jnp.broadcast_to(raw[None], (4, *raw.shape))
    raw = lax.all_to_all(raw, "x", 0, 0, tiled=True)

    steps = [first_step(near[:128], 0), first_step(near[128:], 1)]
    raw, steps, away = lax.optimization_barrier((raw, steps, away))
    mine = [second_step(steps[n], n) for n in range(2)]
    others = [first_step(away[n * 128 : n * 128 + 128], n) for n in range(2)]
    mine, others = lax.optimization_barrier((mine, others))
    mine = mine + paired(mine)
    others = [second_step(others[n], n) for n in range(2)]
    others = others + paired(others)

    picks = raw[:, 3 * QS : 3 * QS + 4].reshape(16, 2, 128)
    picks = jnp.pad(picks, ((0, 0), (0, 6), (0, 0))).reshape(128, 128)
    raw = raw[:, : 3 * QS].reshape(4, 3, QS, ROWS)

    def slot(core):
        first = (jnp.arange(4) - iy + ix) % 4
        first = (first == 0) | (first == (pair(iy, core) - iy) % 4)
        groups = jnp.stack([raw[:, 0], raw[:, 1 + core]], axis=1)
        groups = jnp.where(first[:, None, None, None], groups[..., :128], groups[..., 128:])
        return jnp.concatenate([groups.reshape(8 * QS, 128), picks])

    slots = jnp.stack([slot(0), slot(1)])
    slots = jnp.broadcast_to(slots[None], (4, *slots.shape)).reshape(8, *slots.shape[1:])
    pieces = lax.all_to_all(slots, ("zh", "zl", "core"), 0, 0, tiled=True)

    block_x = jnp.stack([iy - ix, iy - ix + 2, my_pair - ix, my_pair - ix + 2]) % 4
    at = [block_x, block_x, jnp.repeat(jnp.stack([ih, 1 - ih]), 4)]
    at = jnp.concatenate(at + [jnp.stack([iy, my_mate, il * 2 + ic])]).astype(jnp.int32)

    vmem = pl.BlockSpec(memory_space=pltpu.VMEM)
    hilo, norms = pl.pallas_call(
        query_kernel,
        out_shape=(
            jax.ShapeDtypeStruct((4 * GROUP, 1024), BF16),
            jax.ShapeDtypeStruct((2, 8, 128), F32),
        ),
        in_specs=[pl.BlockSpec(memory_space=pltpu.SMEM), vmem],
        out_specs=(vmem, vmem),
        scratch_shapes=[pltpu.VMEM((GROUP, 128), F32)],
        compiler_params=limit(),
        name="query_prepare",
    )(at, pieces)

    tiles = CHUNK // TILE
    cols = [pltpu.VMEM((512, TILE), BF16), pltpu.VMEM((512, TILE), BF16)]
    tile = lambda rows, shift=0: pl.BlockSpec((rows, TILE), lambda t: (0, t + shift))
    partial = pl.pallas_call(
        first_kernel,
        grid=(HALF // TILE,),
        out_shape=jax.ShapeDtypeStruct((2 * GROUP + 8, HALF), F32),
        in_specs=[pl.BlockSpec((4 * GROUP, 512), lambda t: (0, 0))] + [tile(128)] * 4,
        out_specs=tile(2 * GROUP + 8),
        scratch_shapes=cols,
        compiler_params=limit(),
        name="product_first_rows",
    )(hilo, *mine)

    to_mate = lambda x, zh, zl, c, y: (x, zh, zl, c, mate(y, c))
    ends = []
    for n in range(2):
        ours, theirs = pl.pallas_call(
            second_kernel,
            grid=(tiles,),
            out_shape=(jax.ShapeDtypeStruct((GROUP + 8, CHUNK), F32),) * 2,
            in_specs=[
                pl.BlockSpec((4 * GROUP, 512), lambda t: (0, 1)),
                pl.BlockSpec((2, 8, 128), lambda t: (0, 0, 0)),
                tile(2 * GROUP + 8, n * tiles),
            ]
            + [tile(128, n * tiles)] * 4,
            out_specs=(tile(GROUP + 8),) * 2,
            scratch_shapes=cols,
            compiler_params=limit(),
            name="product_other_rows",
        )(hilo, norms, partial, *others)
        ends.append((ours, moved(theirs, to_mate)))

    result = []
    for n in range(2):
        result = pl.pallas_call(
            final_kernel,
            grid=(tiles,),
            out_shape=jax.ShapeDtypeStruct((HALF * 3, 128), F32),
            in_specs=[tile(GROUP + 8)] * 2 + [pl.BlockSpec(memory_space=pl.ANY)] * n,
            out_specs=pl.BlockSpec((TILE * 3, 128), lambda t, n=n: (t + n * tiles, 0)),
            input_output_aliases={2: 0} if n else {},
            compiler_params=limit(),
            name="scale_and_turn",
        )(*ends[n], *([result] if n else []))
    return result.reshape(1, HALF, 1, GROUP)


def solution(mesh):
    fine = Mesh(mesh.devices.reshape(SIZES), AXES)
    rows, ci = ("x", "zh"), ("zl", "core")
    return jax.shard_map(
        shards,
        mesh=fine,
        in_specs=(P(rows, ci + ("y",)), P(ci, None, rows)),
        out_specs=P(ci, rows, "y", None),
        check_vma=False,
    )
```

```python
import functools

import jax
import jax.numpy as jnp
from jax import lax
from jax.experimental import pallas as pl
from jax.experimental.pallas import tpu as pltpu
from jax.sharding import Mesh, PartitionSpec as P

EPS = 1e-6
LIFT = 2.0**40
AXES = ("x", "zh", "zl", "core", "y")
SIZES = (4, 2, 2, 2, 4)
ROWS, COLS, HALF, QS, GROUP = 256, 3072, 1536, 96, 384
CHUNK, TILE = 768, 768
F32, BF16 = jnp.float32, jnp.bfloat16


def pair(k, c):
    return k + 1 - 2 * (k % 2) if c == 0 else 3 - k


def mate(k, c):
    return 3 - k if c == 0 else k + 1 - 2 * (k % 2)


def moved(array, to):
    table = []
    for x in range(4):
        for zh in range(2):
            for zl in range(2):
                for c in range(2):
                    for y in range(4):
                        n = [v % s for v, s in zip(to(x, zh, zl, c, y), SIZES)]
                        table.append((x, zh, zl, c, y, n))
    def index(x, zh, zl, c, y):
        return (((x * 2 + zh) * 2 + zl) * 2 + c) * 4 + y
    return lax.ppermute(array, AXES, [(index(*t[:5]), index(*t[5])) for t in table])


def split(v):
    hi = v.astype(BF16)
    return hi, (v - hi.astype(F32)).astype(BF16)


def query_kernel(at_ref, pieces_ref, hilo_ref, norms_ref, squares_ref):
    total = [[jnp.zeros((QS, 128), F32) for _ in range(4)] for _ in range(2)]
    for b in range(8):
        x, zh = at_ref[b], at_ref[8 + b]
        for g in range(2):
            row = pl.multiple_of(8 * QS + (x * 4 + at_ref[16 + g]) * 8, 8)
            picks = pieces_ref[zh * 4 + at_ref[18], pl.ds(row, 8), :]
            picks = picks[b % 2 : b % 2 + 1, :] * LIFT
            for i in range(4):
                row = pl.multiple_of((x * 2 + g) * QS, 8)
                piece = pieces_ref[zh * 4 + i, pl.ds(row, QS), :]
                total[g][i] = total[g][i] + piece * piece
                hi, lo = split(piece * picks)
                to = g * GROUP + i * QS
                at = (b // 4) * 1536 + (b % 4) * 128
                for n, v in enumerate((hi, lo, hi)):
                    hilo_ref[to : to + QS, at + n * 512 : at + n * 512 + 128] = v
    norms_ref[...] = jnp.zeros_like(norms_ref)
    for g in range(2):
        for i in range(4):
            squares_ref[i * QS : i * QS + QS, :] = total[g][i]
        for j in range(3):
            part = squares_ref[j * 128 : j * 128 + 128, :].T
            norms_ref[g, j + 1 : j + 2, :] = jnp.sum(part, axis=0, keepdims=True)


def products(hilo_ref, blocks, cols):
    squares = jnp.zeros((128, TILE), F32)
    for b, ref in enumerate(blocks):
        v = ref[...]
        squares = squares + v * v
        hi, lo = split(v)
        for n, w in enumerate((hi, hi, lo)):
            cols[n * 512 + b * 128 : n * 512 + b * 128 + 128, :] = w
    value = jnp.dot(hilo_ref[...], cols[...], preferred_element_type=F32)
    return value, jnp.sum(squares, axis=0, keepdims=True)


def first_kernel(hilo_ref, *refs):
    blocks, (out_ref, cols) = refs[:4], refs[4:]
    value, squares = products(hilo_ref, blocks, cols)
    out_ref[: 2 * GROUP, :] = value
    out_ref[2 * GROUP :, :] = jnp.broadcast_to(squares, (8, TILE))


def second_kernel(hilo_ref, norms_ref, before_ref, *refs):
    blocks, (own_ref, other_ref, cols) = refs[:4], refs[4:]
    value, squares = products(hilo_ref, blocks, cols)
    squares = before_ref[2 * GROUP :, :] + squares
    row = lax.broadcasted_iota(jnp.int32, (8, TILE), 0)
    for g, out in ((0, own_ref), (1, other_ref)):
        here = slice(g * GROUP, (g + 1) * GROUP)
        out[:GROUP, :] = before_ref[here, :] + value[here, :]
        norms = jnp.concatenate([norms_ref[g]] * (TILE // 128), axis=1)
        out[GROUP:, :] = jnp.where(row == 0, squares, norms)


def final_kernel(own, got, *refs):
    out_ref = refs[-1]
    squares = own[GROUP:, :] + got[GROUP:, :]
    inverse = 1.0 / jnp.sqrt(squares[:1, :] + EPS)
    value = (own[:GROUP, :] + got[:GROUP, :]) * inverse
    for j in range(3):
        scale = (2.0 / LIFT) / jnp.sqrt(squares[j + 1 : j + 2, :128] + EPS)
        for part in range(TILE // 128):
            block = value[j * 128 : j * 128 + 128, part * 128 : part * 128 + 128]
            out_ref[pl.ds(part * 384 + j, 128, stride=3), :] = block.T * scale


def limit(mib=48):
    return pltpu.CompilerParams(vmem_limit_bytes=mib * 2**20)


def shards(matrix, sample):
    ix, ih, il, ic, iy = (lax.axis_index(a) for a in AXES)
    my_pair = jnp.where(ic == 0, pair(iy, 0), pair(iy, 1))
    my_mate = jnp.where(ic == 0, mate(iy, 0), mate(iy, 1))

    def half_of(side):
        return lax.dynamic_slice(matrix, (0, side * HALF), (ROWS, HALF))

    def first_step(part, n):
        return moved(part, lambda x, zh, zl, c, y: (x, zh, zl, c, y + x + 2 * n))

    def second_step(part, n):
        return moved(part, lambda x, zh, zl, c, y: (y - x - 2 * n, zh, zl, c, y))

    def paired(parts):
        return [moved(p, lambda x, zh, zl, c, y: (x, zh, zl, c, pair(y, c))) for p in parts]

    near, away = half_of(ih), half_of(1 - ih)
    away = moved(away, lambda x, zh, zl, c, y: (x, 1 - zh, zl, c, y))

    raw = jnp.transpose(matrix[:, :QS])
    mates = [moved(raw, lambda x, zh, zl, c, y, k=k: (x, zh, zl, c, mate(y, k))) for k in (0, 1)]
    mates, near = lax.optimization_barrier((mates, near))
    raw = jnp.concatenate([raw, *mates, sample[0].astype(F32), jnp.zeros((4, ROWS), F32)])
    raw = jnp.broadcast_to(raw[None], (4, *raw.shape))
    raw = lax.all_to_all(raw, "x", 0, 0, tiled=True)

    steps = [first_step(near[:128], 0), first_step(near[128:], 1)]
    raw, steps, away = lax.optimization_barrier((raw, steps, away))
    mine = [second_step(steps[n], n) for n in range(2)]
    others = [first_step(away[n * 128 : n * 128 + 128], n) for n in range(2)]
    mine, _ = lax.optimization_barrier((mine, others))
    mine = mine + paired(mine)
    others = [second_step(others[n], n) for n in range(2)]
    others = others + paired(others)

    picks = raw[:, 3 * QS : 3 * QS + 4].reshape(16, 2, 128)
    picks = jnp.pad(picks, ((0, 0), (0, 6), (0, 0))).reshape(128, 128)
    raw = raw[:, : 3 * QS].reshape(4, 3, QS, ROWS)

    def slot(core):
        first = (jnp.arange(4) - iy + ix) % 4
        first = (first == 0) | (first == (pair(iy, core) - iy) % 4)
        groups = jnp.stack([raw[:, 0], raw[:, 1 + core]], axis=1)
        groups = jnp.where(first[:, None, None, None], groups[..., :128], groups[..., 128:])
        return jnp.concatenate([groups.reshape(8 * QS, 128), picks])

    slots = jnp.stack([slot(0), slot(1)])
    slots = jnp.broadcast_to(slots[None], (4, *slots.shape)).reshape(8, *slots.shape[1:])
    pieces = lax.all_to_all(slots, ("zh", "zl", "core"), 0, 0, tiled=True)

    block_x = jnp.stack([iy - ix, iy - ix + 2, my_pair - ix, my_pair - ix + 2]) % 4
    at = [block_x, block_x, jnp.repeat(jnp.stack([ih, 1 - ih]), 4)]
    at = jnp.concatenate(at + [jnp.stack([iy, my_mate, il * 2 + ic])]).astype(jnp.int32)

    vmem = pl.BlockSpec(memory_space=pltpu.VMEM)
    hilo, norms = pl.pallas_call(
        query_kernel,
        out_shape=(
            jax.ShapeDtypeStruct((2 * GROUP, 3072), BF16),
            jax.ShapeDtypeStruct((2, 8, 128), F32),
        ),
        in_specs=[pl.BlockSpec(memory_space=pltpu.SMEM), vmem],
        out_specs=(vmem, vmem),
        scratch_shapes=[pltpu.VMEM((GROUP, 128), F32)],
        compiler_params=limit(),
        name="query_prepare",
    )(at, pieces)

    tiles = CHUNK // TILE
    cols = [pltpu.VMEM((1536, TILE), BF16)]
    tile = lambda rows, shift=0: pl.BlockSpec((rows, TILE), lambda t: (0, t + shift))
    partial = pl.pallas_call(
        first_kernel,
        grid=(HALF // TILE,),
        out_shape=jax.ShapeDtypeStruct((2 * GROUP + 8, HALF), F32),
        in_specs=[pl.BlockSpec((2 * GROUP, 1536), lambda t: (0, 0))] + [tile(128)] * 4,
        out_specs=tile(2 * GROUP + 8),
        scratch_shapes=cols,
        compiler_params=limit(),
        name="product_first_rows",
    )(hilo, *mine)

    to_mate = lambda x, zh, zl, c, y: (x, zh, zl, c, mate(y, c))
    ends = []
    for n in range(2):
        ours, theirs = pl.pallas_call(
            second_kernel,
            grid=(tiles,),
            out_shape=(jax.ShapeDtypeStruct((GROUP + 8, CHUNK), F32),) * 2,
            in_specs=[
                pl.BlockSpec((2 * GROUP, 1536), lambda t: (0, 1)),
                pl.BlockSpec((2, 8, 128), lambda t: (0, 0, 0)),
                tile(2 * GROUP + 8, n * tiles),
            ]
            + [tile(128, n * tiles)] * 4,
            out_specs=(tile(GROUP + 8),) * 2,
            scratch_shapes=cols,
            compiler_params=limit(),
            name="product_other_rows",
        )(hilo, norms, partial, *others)
        ends.append((ours, moved(theirs, to_mate)))

    result = []
    for n in range(2):
        result = pl.pallas_call(
            final_kernel,
            grid=(tiles,),
            out_shape=jax.ShapeDtypeStruct((HALF * 3, 128), F32),
            in_specs=[tile(GROUP + 8)] * 2 + [pl.BlockSpec(memory_space=pl.ANY)] * n,
            out_specs=pl.BlockSpec((TILE * 3, 128), lambda t, n=n: (t + n * tiles, 0)),
            input_output_aliases={2: 0} if n else {},
            compiler_params=limit(),
            name="scale_and_turn",
        )(*ends[n], *([result] if n else []))
    return result.reshape(1, HALF, 1, GROUP)


def solution(mesh):
    fine = Mesh(mesh.devices.reshape(SIZES), AXES)
    rows, ci = ("x", "zh"), ("zl", "core")
    return jax.shard_map(
        shards,
        mesh=fine,
        in_specs=(P(rows, ci + ("y",)), P(ci, None, rows)),
        out_specs=P(ci, rows, "y", None),
        check_vma=False,
    )
```

```python
import functools

import jax
import jax.numpy as jnp
from jax import lax
from jax.experimental import pallas as pl
from jax.experimental.pallas import tpu as pltpu
from jax.sharding import Mesh, PartitionSpec as P

EPS = 1e-6
LIFT = 2.0**40
AXES = ("x", "zh", "zl", "core", "y")
SIZES = (4, 2, 2, 2, 4)
ROWS, COLS, HALF, QS, GROUP = 256, 3072, 1536, 96, 384
CHUNK, TILE = 512, 512
F32, BF16 = jnp.float32, jnp.bfloat16


def pair(k, c):
    return k + 1 - 2 * (k % 2) if c == 0 else 3 - k


def mate(k, c):
    return 3 - k if c == 0 else k + 1 - 2 * (k % 2)


def moved(array, to):
    table = []
    for x in range(4):
        for zh in range(2):
            for zl in range(2):
                for c in range(2):
                    for y in range(4):
                        n = [v % s for v, s in zip(to(x, zh, zl, c, y), SIZES)]
                        table.append((x, zh, zl, c, y, n))
    def index(x, zh, zl, c, y):
        return (((x * 2 + zh) * 2 + zl) * 2 + c) * 4 + y
    return lax.ppermute(array, AXES, [(index(*t[:5]), index(*t[5])) for t in table])


def split(v):
    hi = v.astype(BF16)
    return hi, (v - hi.astype(F32)).astype(BF16)


def query_kernel(at_ref, pieces_ref, hilo_ref, norms_ref, squares_ref):
    total = [[jnp.zeros((QS, 128), F32) for _ in range(4)] for _ in range(2)]
    for b in range(8):
        x, zh = at_ref[b], at_ref[8 + b]
        for g in range(2):
            row = pl.multiple_of(8 * QS + (x * 4 + at_ref[16 + g]) * 8, 8)
            picks = pieces_ref[zh * 4 + at_ref[18], pl.ds(row, 8), :]
            picks = picks[b % 2 : b % 2 + 1, :] * LIFT
            for i in range(4):
                row = pl.multiple_of((x * 2 + g) * QS, 8)
                piece = pieces_ref[zh * 4 + i, pl.ds(row, QS), :]
                total[g][i] = total[g][i] + piece * piece
                hi, lo = split(piece * picks)
                to = g * GROUP + i * QS
                at = (b // 4) * 1536 + (b % 4) * 128
                for n, v in enumerate((hi, lo, hi)):
                    hilo_ref[to : to + QS, at + n * 512 : at + n * 512 + 128] = v
    norms_ref[...] = jnp.zeros_like(norms_ref)
    for g in range(2):
        for i in range(4):
            squares_ref[i * QS : i * QS + QS, :] = total[g][i]
        for j in range(3):
            part = squares_ref[j * 128 : j * 128 + 128, :].T
            norms_ref[g, j + 1 : j + 2, :] = jnp.sum(part, axis=0, keepdims=True)


def products(hilo_ref, blocks, cols):
    squares = jnp.zeros((128, TILE), F32)
    for b, ref in enumerate(blocks):
        v = ref[...]
        squares = squares + v * v
        hi, lo = split(v)
        for n, w in enumerate((hi, hi, lo)):
            cols[n * 512 + b * 128 : n * 512 + b * 128 + 128, :] = w
    value = jnp.dot(hilo_ref[...], cols[...], preferred_element_type=F32)
    return value, jnp.sum(squares, axis=0, keepdims=True)


def first_kernel(hilo_ref, *refs):
    blocks, (out_ref, cols) = refs[:4], refs[4:]
    value, squares = products(hilo_ref, blocks, cols)
    out_ref[: 2 * GROUP, :] = value
    out_ref[2 * GROUP :, :] = jnp.broadcast_to(squares, (8, TILE))


def second_kernel(hilo_ref, norms_ref, before_ref, *refs):
    blocks, (own_ref, other_ref, cols) = refs[:4], refs[4:]
    value, squares = products(hilo_ref, blocks, cols)
    squares = before_ref[2 * GROUP :, :] + squares
    row = lax.broadcasted_iota(jnp.int32, (8, TILE), 0)
    for g, out in ((0, own_ref), (1, other_ref)):
        here = slice(g * GROUP, (g + 1) * GROUP)
        out[:GROUP, :] = before_ref[here, :] + value[here, :]
        norms = jnp.concatenate([norms_ref[g]] * (TILE // 128), axis=1)
        out[GROUP:, :] = jnp.where(row == 0, squares, norms)


def final_kernel(own, got, *refs):
    out_ref = refs[-1]
    squares = own[GROUP:, :] + got[GROUP:, :]
    inverse = 1.0 / jnp.sqrt(squares[:1, :] + EPS)
    value = (own[:GROUP, :] + got[:GROUP, :]) * inverse
    for j in range(3):
        scale = (2.0 / LIFT) / jnp.sqrt(squares[j + 1 : j + 2, :128] + EPS)
        for part in range(TILE // 128):
            block = value[j * 128 : j * 128 + 128, part * 128 : part * 128 + 128]
            out_ref[pl.ds(part * 384 + j, 128, stride=3), :] = block.T * scale


def limit(mib=48):
    return pltpu.CompilerParams(vmem_limit_bytes=mib * 2**20)


def shards(matrix, sample):
    ix, ih, il, ic, iy = (lax.axis_index(a) for a in AXES)
    my_pair = jnp.where(ic == 0, pair(iy, 0), pair(iy, 1))
    my_mate = jnp.where(ic == 0, mate(iy, 0), mate(iy, 1))

    def half_of(side):
        return lax.dynamic_slice(matrix, (0, side * HALF), (ROWS, HALF))

    def first_step(part, n):
        return moved(part, lambda x, zh, zl, c, y: (x, zh, zl, c, y + x + 2 * n))

    def second_step(part, n):
        return moved(part, lambda x, zh, zl, c, y: (y - x - 2 * n, zh, zl, c, y))

    def paired(parts):
        return [moved(p, lambda x, zh, zl, c, y: (x, zh, zl, c, pair(y, c))) for p in parts]

    near, away = half_of(ih), half_of(1 - ih)
    away = moved(away, lambda x, zh, zl, c, y: (x, 1 - zh, zl, c, y))

    raw = jnp.transpose(matrix[:, :QS])
    mates = [moved(raw, lambda x, zh, zl, c, y, k=k: (x, zh, zl, c, mate(y, k))) for k in (0, 1)]
    mates, near = lax.optimization_barrier((mates, near))
    raw = jnp.concatenate([raw, *mates, sample[0].astype(F32), jnp.zeros((4, ROWS), F32)])
    raw = jnp.broadcast_to(raw[None], (4, *raw.shape))
    raw = lax.all_to_all(raw, "x", 0, 0, tiled=True)

    steps = [first_step(near[:128], 0), first_step(near[128:], 1)]
    raw, steps, away = lax.optimization_barrier((raw, steps, away))
    mine = [second_step(steps[n], n) for n in range(2)]
    others = [first_step(away[n * 128 : n * 128 + 128], n) for n in range(2)]
    mine, _ = lax.optimization_barrier((mine, others))
    mine = mine + paired(mine)
    others = [second_step(others[n], n) for n in range(2)]
    others = others + paired(others)

    picks = raw[:, 3 * QS : 3 * QS + 4].reshape(16, 2, 128)
    picks = jnp.pad(picks, ((0, 0), (0, 6), (0, 0))).reshape(128, 128)
    raw = raw[:, : 3 * QS].reshape(4, 3, QS, ROWS)

    def slot(core):
        first = (jnp.arange(4) - iy + ix) % 4
        first = (first == 0) | (first == (pair(iy, core) - iy) % 4)
        groups = jnp.stack([raw[:, 0], raw[:, 1 + core]], axis=1)
        groups = jnp.where(first[:, None, None, None], groups[..., :128], groups[..., 128:])
        return jnp.concatenate([groups.reshape(8 * QS, 128), picks])

    slots = jnp.stack([slot(0), slot(1)])
    slots = jnp.broadcast_to(slots[None], (4, *slots.shape)).reshape(8, *slots.shape[1:])
    pieces = lax.all_to_all(slots, ("zh", "zl", "core"), 0, 0, tiled=True)

    block_x = jnp.stack([iy - ix, iy - ix + 2, my_pair - ix, my_pair - ix + 2]) % 4
    at = [block_x, block_x, jnp.repeat(jnp.stack([ih, 1 - ih]), 4)]
    at = jnp.concatenate(at + [jnp.stack([iy, my_mate, il * 2 + ic])]).astype(jnp.int32)

    vmem = pl.BlockSpec(memory_space=pltpu.VMEM)
    hilo, norms = pl.pallas_call(
        query_kernel,
        out_shape=(
            jax.ShapeDtypeStruct((2 * GROUP, 3072), BF16),
            jax.ShapeDtypeStruct((2, 8, 128), F32),
        ),
        in_specs=[pl.BlockSpec(memory_space=pltpu.SMEM), vmem],
        out_specs=(vmem, vmem),
        scratch_shapes=[pltpu.VMEM((GROUP, 128), F32)],
        compiler_params=limit(),
        name="query_prepare",
    )(at, pieces)

    tiles = CHUNK // TILE
    cols = [pltpu.VMEM((1536, TILE), BF16)]
    tile = lambda rows, shift=0: pl.BlockSpec((rows, TILE), lambda t: (0, t + shift))
    partial = pl.pallas_call(
        first_kernel,
        grid=(HALF // TILE,),
        out_shape=jax.ShapeDtypeStruct((2 * GROUP + 8, HALF), F32),
        in_specs=[pl.BlockSpec((2 * GROUP, 1536), lambda t: (0, 0))] + [tile(128)] * 4,
        out_specs=tile(2 * GROUP + 8),
        scratch_shapes=cols,
        compiler_params=limit(),
        name="product_first_rows",
    )(hilo, *mine)

    to_mate = lambda x, zh, zl, c, y: (x, zh, zl, c, mate(y, c))
    ends = []
    for n in range(HALF // CHUNK):
        ours, theirs = pl.pallas_call(
            second_kernel,
            grid=(tiles,),
            out_shape=(jax.ShapeDtypeStruct((GROUP + 8, CHUNK), F32),) * 2,
            in_specs=[
                pl.BlockSpec((2 * GROUP, 1536), lambda t: (0, 1)),
                pl.BlockSpec((2, 8, 128), lambda t: (0, 0, 0)),
                tile(2 * GROUP + 8, n * tiles),
            ]
            + [tile(128, n * tiles)] * 4,
            out_specs=(tile(GROUP + 8),) * 2,
            scratch_shapes=cols,
            compiler_params=limit(),
            name="product_other_rows",
        )(hilo, norms, partial, *others)
        ends.append((ours, moved(theirs, to_mate)))

    result = []
    for n in range(HALF // CHUNK):
        result = pl.pallas_call(
            final_kernel,
            grid=(tiles,),
            out_shape=jax.ShapeDtypeStruct((HALF * 3, 128), F32),
            in_specs=[tile(GROUP + 8)] * 2 + [pl.BlockSpec(memory_space=pl.ANY)] * (n > 0),
            out_specs=pl.BlockSpec((TILE * 3, 128), lambda t, n=n: (t + n * tiles, 0)),
            input_output_aliases={2: 0} if n else {},
            compiler_params=limit(),
            name="scale_and_turn",
        )(*ends[n], *([result] if n else []))
    return result.reshape(1, HALF, 1, GROUP)


def solution(mesh):
    fine = Mesh(mesh.devices.reshape(SIZES), AXES)
    rows, ci = ("x", "zh"), ("zl", "core")
    return jax.shard_map(
        shards,
        mesh=fine,
        in_specs=(P(rows, ci + ("y",)), P(ci, None, rows)),
        out_specs=P(ci, rows, "y", None),
        check_vma=False,
    )
```
